32 devices in a mesh: layer: 4 (over z), latent: 8 (over y, x, core).
Axes of the slice: x: 2, y: 2, z: 4, core: 2. Of those that a mesh axis runs over, the one named last changes fastest.
Arguments:
- resid: bfloat16 [4, 256, 4096], P('layer', 'latent'), may hold values from -6 to 6
- mlp_out: bfloat16 [4, 256, 4096], P('layer', 'latent'), may hold values from -6 to 6
- enc_w: bfloat16 [4, 4096, 4096], P('layer', None, 'latent'), may hold values from -0.09375 to 0.09375
- enc_b: float32 [4, 4096], P('layer', 'latent'), may hold values from -3 to 3
- dec_w: bfloat16 [4, 4, 4096, 4096], P('layer', None, 'latent'), may hold values from -0.046875 to 0.046875
Outputs:
- error: bfloat16 [4, 256, 4096], P('layer', 'latent')
The draws below stay inside these ranges and needn't reach their ends.
All inputs are finite; a program needn't handle non-finite values.
Results may differ from the reference program's by a relative error of at most 0.0034.
Values may be sent and summed in bfloat16 or wider, within the bound.
No kernel may reach another device: no remote copies, remote signals or barrier semaphores. Data moves between devices by JAX's collectives and lax.ppermute only.
A program may use at most 128 MiB of HBM per device.

```python
import jax
import jax.numpy as jnp

D = 4096
F = 4096
LAYERS = 4
TOKENS = 256


def shard_levels(stream_key, dims, shards, low, largest):
    factor_of = 1.0
    for dim, blocks in shards:
        draws = jax.random.uniform(jax.random.fold_in(jax.random.fold_in(stream_key, 6), dim), (blocks,), jnp.float32, low / len(shards), largest / len(shards))
        factor_of = factor_of * jnp.repeat(jnp.exp(draws), dims[dim] // blocks).reshape((-1,) + (1,) * (len(dims) - 1 - dim))
    return factor_of


def noise(rng, dims, deviation, reach, cuts=(), held_as=jnp.bfloat16):
    factor_of = shard_levels(rng, dims, cuts, -0.22, 0.18) if cuts else 1.0
    drawn = jax.random.normal(rng, dims, jnp.float32) * deviation * factor_of
    return jnp.minimum(jnp.maximum(drawn, -reach), reach).astype(held_as)


def setup_inputs(seed: int = 0) -> dict:
    splits = jax.random.split(jax.random.key(seed), 6)
    resid = noise(splits[0], (LAYERS, TOKENS, D), 1.0, 6.0, ((0, 4), (1, 8)))
    mlp_out = noise(splits[1], (LAYERS, TOKENS, D), 1.0, 6.0, ((0, 4), (1, 8)))
    enc_w = noise(splits[2], (LAYERS, D, F), D ** -0.5, 0.09375, ((0, 4), (2, 8)))
    enc_b = noise(splits[3], (LAYERS, F), 0.5, 3.0, ((0, 4), (1, 8)), jnp.float32)
    dec_w = noise(splits[4], (LAYERS, LAYERS, F, D), (LAYERS * F) ** -0.5, 0.046875, ((0, 4), (2, 8)))
    return {"resid": resid, "mlp_out": mlp_out, "enc_w": enc_w, "enc_b": enc_b, "dec_w": dec_w}


def reference(resid, mlp_out, enc_w, enc_b, dec_w):
    latents = []
    for source in range(LAYERS):
        pre = jnp.dot(resid[source], enc_w[source], preferred_element_type=jnp.float32) + enc_b[source]
        latents.append(jnp.maximum(pre, 0.0).astype(jnp.bfloat16))
    errors = []
    for target in range(LAYERS):
        recon = jnp.zeros((TOKENS, D), jnp.float32)
        for source in range(target + 1):
            recon = recon + jnp.dot(latents[source], dec_w[target, source], preferred_element_type=jnp.float32)
        errors.append((mlp_out[target].astype(jnp.float32) - recon).astype(jnp.bfloat16))
    return jnp.stack(errors)
```

```python
import functools

import jax
import jax.numpy as jnp
from jax import lax
from jax.experimental import pallas as pl
from jax.experimental.pallas import tpu as pltpu
from jax.sharding import PartitionSpec as P

F32 = jnp.float32
BF16 = jnp.bfloat16
LIMIT = 48 * 1024 * 1024


def swap(shard, even_mask, odd_mask):
    peers = lax.axis_size("latent")
    pairs = [(i, i ^ (odd_mask if i & 1 else even_mask)) for i in range(peers)]
    return lax.ppermute(shard, "latent", pairs)


def up(shard):
    layers = lax.axis_size("layer")
    return lax.ppermute(shard, "layer", [(i, i + 1) for i in range(layers - 1)])


def tile_of(total, most):
    tile = min(total, most)
    while total % tile:
        tile //= 2
    return tile


def encode_kernel(top_ref, low_ref, w_ref, b_ref, out_ref, acc_ref):
    k = pl.program_id(0)
    half = top_ref.shape[0]

    @pl.when(k == 0)
    def _():
        acc_ref[...] = jnp.zeros_like(acc_ref)

    acc_ref[:half] += jnp.dot(top_ref[...], w_ref[...], preferred_element_type=F32)
    acc_ref[half:] += jnp.dot(low_ref[...], w_ref[...], preferred_element_type=F32)

    @pl.when(k == pl.num_programs(0) - 1)
    def _():
        out_ref[...] = jnp.maximum(acc_ref[...] + b_ref[...], 0.0).astype(BF16)


def encode(top, low, w, b):
    half, depth = top.shape
    wide = w.shape[1]
    tk = tile_of(depth, 512)
    return pl.pallas_call(
        encode_kernel,
        grid=(depth // tk,),
        in_specs=[
            pl.BlockSpec((half, tk), lambda k: (0, k)),
            pl.BlockSpec((half, tk), lambda k: (0, k)),
            pl.BlockSpec((tk, wide), lambda k: (k, 0)),
            pl.BlockSpec((1, wide), lambda k: (0, 0)),
        ],
        out_specs=pl.BlockSpec((2 * half, wide), lambda k: (0, 0)),
        out_shape=jax.ShapeDtypeStruct((2 * half, wide), BF16),
        scratch_shapes=[pltpu.VMEM((2 * half, wide), F32)],
        compiler_params=pltpu.CompilerParams(vmem_limit_bytes=LIMIT),
        cost_estimate=pl.CostEstimate(
            flops=4 * half * depth * wide,
            bytes_accessed=2 * depth * wide + 4 * half * depth,
            transcendentals=0,
        ),
    )(top, low, w, b)


def decode_kernel(count, last, target_ref, *refs):
    lats, weights = refs[:count], refs[count : 2 * count]
    rest = refs[2 * count :]
    total = jnp.dot(lats[0][...], weights[0][0], preferred_element_type=F32)
    for lat, w in zip(lats[1:], weights[1:]):
        total += jnp.dot(lat[...], w[0], preferred_element_type=F32)
    if last:
        acc_ref, top_ref, low_ref = rest
        total += acc_ref[...]
        half = top_ref.shape[0]
        top_ref[...] = total[:half]
        low_ref[...] = total[half:].astype(BF16)
    else:
        rest[-1][...] = total


def decode(lats, first, target, weights, acc=None):
    count = len(lats)
    rows, depth = lats[0].shape
    wide = weights.shape[2]
    tn = tile_of(wide, 512)

    def at(j):
        return lambda n, t: (jnp.maximum(t[0] - (first + j), 0), 0, n)

    block = pl.BlockSpec((rows, tn), lambda n, t: (0, n))
    half = pl.BlockSpec((rows // 2, tn), lambda n, t: (0, n))
    last = acc is not None
    return pl.pallas_call(
        functools.partial(decode_kernel, count, last),
        grid_spec=pltpu.PrefetchScalarGridSpec(
            num_scalar_prefetch=1,
            grid=(wide // tn,),
            in_specs=[pl.BlockSpec((rows, depth), lambda n, t: (0, 0))] * count
            + [pl.BlockSpec((1, depth, tn), at(j)) for j in range(count)]
            + ([block] if last else []),
            out_specs=[half, half] if last else block,
        ),
        out_shape=[
            jax.ShapeDtypeStruct((rows // 2, wide), F32),
            jax.ShapeDtypeStruct((rows // 2, wide), BF16),
        ]
        if last
        else jax.ShapeDtypeStruct((rows, wide), F32),
        compiler_params=pltpu.CompilerParams(vmem_limit_bytes=LIMIT),
        cost_estimate=pl.CostEstimate(
            flops=2 * count * rows * depth * wide,
            bytes_accessed=2 * count * depth * wide + 8 * rows * wide,
            transcendentals=0,
        ),
    )(target, *lats, *([weights] * count), *([acc] if last else []))


def body(resid, mlp_out, enc_w, enc_b, dec_w):
    target = lax.axis_index("layer").reshape(1)
    layers = lax.axis_size("layer")
    peers = lax.axis_size("latent")
    weights = dec_w[0]
    masks = [1 << bit for bit in range(1, peers.bit_length() - 1)]
    steps = list(zip(masks, masks[::-1]))

    held = resid[0]
    for even, odd in steps:
        held = jnp.concatenate([held, swap(held, even, odd)], 0)
    carried = encode(held, swap(held, 1, 1), enc_w[0], enc_b)

    lats = [carried]
    for _ in range(layers - 2):
        carried = up(carried)
        lats.append(carried)
    final = up(carried)
    early = decode(lats, 0, target, weights)
    top, low = decode([final], layers - 1, target, weights, early)

    total = top + swap(low, 1, 1).astype(F32)
    for even, odd in steps[::-1]:
        half = total.shape[0] // 2
        total = total[:half] + swap(total[half:].astype(BF16), even, odd).astype(F32)
    return (mlp_out[0].astype(F32) - total).astype(BF16)[None]


def solution(mesh):
    return jax.shard_map(
        body,
        mesh=mesh,
        in_specs=(
            P("layer", "latent", None),
            P("layer", "latent", None),
            P("layer", None, "latent"),
            P("layer", "latent"),
            P("layer", None, "latent", None),
        ),
        out_specs=P("layer", "latent", None),
        check_vma=False,
    )
```

```python
import functools

import jax
import jax.numpy as jnp
from jax import lax
from jax.experimental import pallas as pl
from jax.experimental.pallas import tpu as pltpu
from jax.sharding import PartitionSpec as P

F32 = jnp.float32
BF16 = jnp.bfloat16
MIB = 1024 * 1024
WHOLE = pl.BlockSpec(memory_space=pltpu.VMEM)
FAR = pl.BlockSpec(memory_space=pltpu.HBM)
SCALAR = pl.BlockSpec(memory_space=pltpu.SMEM)


def swap(shard, masks):
    peers = lax.axis_size("latent")
    return lax.ppermute(shard, "latent", [(i, i ^ masks[i & 1]) for i in range(peers)])


def up(shard, by, back):
    layers = lax.axis_size("layer")
    return lax.ppermute(shard, "layer", [(i - by, i) for i in range(back, layers)])


def after(value, *others):
    return lax.optimization_barrier((value, *others))[0]


def tile_of(total, most):
    tile = min(total, most)
    while total % tile:
        tile //= 2
    return tile


def run_all(copies):
    for copy in copies:
        copy.start()
    for copy in copies:
        copy.wait()


def load_kernel(count, cuts, *refs):
    srcs, dsts, sems = refs[:count], refs[count : 2 * count], refs[2 * count]
    copies = []
    for n, (src, dst, cut) in enumerate(zip(srcs, dsts, cuts)):
        rows = src.shape[0] // cut
        for i in range(cut):
            part = pl.ds(i * rows, rows)
            copies.append(pltpu.make_async_copy(src.at[part], dst.at[part], sems.at[sum(cuts[:n]) + i]))
    run_all(copies)


def load(arrays, cuts):
    count = len(arrays)
    return pl.pallas_call(
        functools.partial(load_kernel, count, cuts),
        in_specs=[FAR] * count,
        out_specs=[WHOLE] * count,
        out_shape=[pltpu.VMEM(a.shape, a.dtype) for a in arrays],
        scratch_shapes=[pltpu.SemaphoreType.DMA((sum(cuts),))],
        compiler_params=pltpu.CompilerParams(vmem_limit_bytes=2 * MIB),
        cost_estimate=pl.CostEstimate(flops=1024, bytes_accessed=1024, transcendentals=0),
    )(*[pltpu.with_memory_space_constraint(a, pltpu.HBM) for a in arrays])


def pick_kernel(cuts, target_ref, src_ref, *refs):
    dsts, sems = refs[:-1], refs[-1]
    rows = dsts[0].shape[0] // cuts
    copies = []
    for back, dst_ref in enumerate(dsts):
        source = jnp.maximum(target_ref[0] - back, 0)
        for i in range(cuts):
            part = pl.ds(i * rows, rows)
            copies.append(pltpu.make_async_copy(src_ref.at[source, part], dst_ref.at[part], sems.at[back, i]))
    run_all(copies)


def pick(weights, target):
    count, depth, wide = weights.shape
    cuts = 2
    return pl.pallas_call(
        functools.partial(pick_kernel, cuts),
        in_specs=[SCALAR, FAR],
        out_specs=[WHOLE] * count,
        out_shape=[pltpu.VMEM((depth, wide), weights.dtype)] * count,
        scratch_shapes=[pltpu.SemaphoreType.DMA((count, cuts))],
        compiler_params=pltpu.CompilerParams(vmem_limit_bytes=2 * MIB),
        cost_estimate=pl.CostEstimate(flops=1024, bytes_accessed=1024, transcendentals=0),
    )(target, pltpu.with_memory_space_constraint(weights, pltpu.HBM))


def encode_kernel(count, *refs):
    pieces, (w_ref, b_ref, out_ref) = refs[:count], refs[count:]
    rows = jnp.concatenate([piece[...] for piece in pieces], 0)
    pre = jnp.dot(rows, w_ref[...], preferred_element_type=F32) + b_ref[...]
    out_ref[...] = jnp.maximum(pre, 0.0).astype(BF16)


def encode(pieces, w, b):
    count = len(pieces)
    rows = sum(piece.shape[0] for piece in pieces)
    depth, wide = w.shape
    return pl.pallas_call(
        functools.partial(encode_kernel, count),
        in_specs=[WHOLE] * (count + 2),
        out_specs=WHOLE,
        out_shape=pltpu.VMEM((rows, wide), BF16),
        compiler_params=pltpu.CompilerParams(vmem_limit_bytes=16 * MIB),
        cost_estimate=pl.CostEstimate(flops=1024, bytes_accessed=1024, transcendentals=0),
    )(*pieces, w, b)


def decode_kernel(count, tile, summed, halved, *refs):
    lats, ws, rest = refs[:count], refs[count : 2 * count], refs[2 * count :]
    wide = ws[0].shape[1]

    @pl.loop(0, wide // tile)
    def _(n):
        columns = pl.ds(pl.multiple_of(n * tile, tile), tile)
        total = jnp.dot(lats[0][...], ws[0][:, columns], preferred_element_type=F32)
        for lat, w in zip(lats[1:], ws[1:]):
            total += jnp.dot(lat[...], w[:, columns], preferred_element_type=F32)
        if summed:
            total += rest[0][:, columns]
        if halved:
            top_ref, low_ref = rest[-2:]
            half = top_ref.shape[0]
            top_ref[:, columns] = total[:half]
            low_ref[:, columns] = total[half:].astype(BF16)
        else:
            rest[-1][:, columns] = total


def decode(lats, weights, acc=None, halved=False):
    count = len(lats)
    rows, depth = lats[0].shape
    wide = weights[0].shape[1]
    summed = acc is not None
    halves = [pltpu.VMEM((rows // 2, wide), F32), pltpu.VMEM((rows // 2, wide), BF16)]
    return pl.pallas_call(
        functools.partial(decode_kernel, count, tile_of(wide, 2048), summed, halved),
        in_specs=[WHOLE] * (2 * count + summed),
        out_specs=[WHOLE, WHOLE] if halved else WHOLE,
        out_shape=halves if halved else pltpu.VMEM((rows, wide), F32),
        compiler_params=pltpu.CompilerParams(vmem_limit_bytes=8 * MIB),
        cost_estimate=pl.CostEstimate(flops=1024, bytes_accessed=1024, transcendentals=0),
    )(*lats, *weights, *([acc] if summed else []))


def body(resid, mlp_out, enc_w, enc_b, dec_w):
    target = lax.axis_index("layer").reshape(1)
    layers = lax.axis_size("layer")
    peers = lax.axis_size("latent")
    bits = [1 << bit for bit in range(1, peers.bit_length() - 1)]
    steps = list(zip(bits, bits[::-1]))

    pieces = [resid[0]]
    for masks in steps:
        pieces += [swap(piece, masks) for piece in pieces]
    count = len(pieces)
    half = count // 2
    encoder, bias, mine = load([after(enc_w[0], pieces[half]), enc_b, resid[0]], [4, 1, 1])
    pieces[-1] = after(pieces[-1], encoder)
    mates = [swap(piece, (1, 1)) for piece in pieces]
    pieces[0] = mine

    def gather(group, *gate):
        return encode([after(pieces[i], *gate) for i in group] + [mates[i] for i in group], encoder, bias)

    def lift(held, *gate):
        for j in range(len(held), layers):
            held.append(up(after(held[j - 1], *gate) if j > 2 else held[j - 1], 1, j) if j % 2 else up(held[j - 2], 2, j))

    far = [gather(range(half, count))]
    near = [gather(range(half), far[0])]
    weights = pick(after(dec_w[0], near[0]), target)
    lift(far, weights[0])
    lift(near, weights[0])
    sums = [decode([after(lat, near[2]) for lat in held[:-1]], weights[:-1]) for held in (far, near)]
    top, low = decode([after(far[-1], near[-1], sums[1])], weights[-1:], sums[0], True)
    ends = [top + swap(low, (1, 1)).astype(F32)]
    top, low = decode([after(near[-1], low)], weights[-1:], sums[1], True)
    ends.insert(0, top + swap(low, (1, 1)).astype(F32))
    each = resid.shape[1]
    totals = [end[i * each : (i + 1) * each] for end in ends for i in range(half)]
    for masks in steps[::-1]:
        half = len(totals) // 2
        for i in reversed(range(half)):
            totals[i] = totals[i] + swap(totals[half + i].astype(BF16), masks).astype(F32)
        totals = totals[:half]
    return (mlp_out[0].astype(F32) - totals[0]).astype(BF16)[None]


def solution(mesh):
    return jax.shard_map(
        body,
        mesh=mesh,
        in_specs=(
            P("layer", "latent", None),
            P("layer", "latent", None),
            P("layer", None, "latent"),
            P("layer", "latent"),
            P("layer", None, "latent", None),
        ),
        out_specs=P("layer", "latent", None),
        check_vma=False,
    )
```

```python
import functools

import jax
import jax.numpy as jnp
from jax import lax
from jax.experimental import pallas as pl
from jax.experimental.pallas import tpu as pltpu
from jax.sharding import PartitionSpec as P

F32 = jnp.float32
BF16 = jnp.bfloat16
MIB = 1024 * 1024
WHOLE = pl.BlockSpec(memory_space=pltpu.VMEM)
FAR = pl.BlockSpec(memory_space=pltpu.HBM)
SCALAR = pl.BlockSpec(memory_space=pltpu.SMEM)


def swap(shard, masks):
    peers = lax.axis_size("latent")
    return lax.ppermute(shard, "latent", [(i, i ^ masks[i & 1]) for i in range(peers)])


def up(shard, by, back):
    layers = lax.axis_size("layer")
    return lax.ppermute(shard, "layer", [(i - by, i) for i in range(back, layers)])


def after(value, *others):
    return lax.optimization_barrier((value, *others))[0]


def tile_of(total, most):
    tile = min(total, most)
    while total % tile:
        tile //= 2
    return tile


def run_all(copies):
    for copy in copies:
        copy.start()
    for copy in copies:
        copy.wait()


def load_kernel(count, cuts, *refs):
    srcs, dsts, sems = refs[:count], refs[count : 2 * count], refs[2 * count]
    copies = []
    for n, (src, dst, cut) in enumerate(zip(srcs, dsts, cuts)):
        rows = src.shape[0] // cut
        for i in range(cut):
            part = pl.ds(i * rows, rows)
            copies.append(pltpu.make_async_copy(src.at[part], dst.at[part], sems.at[sum(cuts[:n]) + i]))
    run_all(copies)


def load(arrays, cuts):
    count = len(arrays)
    return pl.pallas_call(
        functools.partial(load_kernel, count, cuts),
        in_specs=[FAR] * count,
        out_specs=[WHOLE] * count,
        out_shape=[pltpu.VMEM(a.shape, a.dtype) for a in arrays],
        scratch_shapes=[pltpu.SemaphoreType.DMA((sum(cuts),))],
        compiler_params=pltpu.CompilerParams(vmem_limit_bytes=2 * MIB),
        cost_estimate=pl.CostEstimate(flops=1024, bytes_accessed=1024, transcendentals=0),
    )(*[pltpu.with_memory_space_constraint(a, pltpu.HBM) for a in arrays])


def pick_kernel(cuts, target_ref, src_ref, *refs):
    dsts, sems = refs[:-1], refs[-1]
    rows = dsts[0].shape[0] // cuts
    copies = []
    for back, dst_ref in enumerate(dsts):
        source = jnp.maximum(target_ref[0] - back, 0)
        for i in range(cuts):
            part = pl.ds(i * rows, rows)
            copies.append(pltpu.make_async_copy(src_ref.at[source, part], dst_ref.at[part], sems.at[back, i]))
    run_all(copies)


def pick(weights, target):
    count, depth, wide = weights.shape
    cuts = 4
    return pl.pallas_call(
        functools.partial(pick_kernel, cuts),
        in_specs=[SCALAR, FAR],
        out_specs=[WHOLE] * count,
        out_shape=[pltpu.VMEM((depth, wide), weights.dtype)] * count,
        scratch_shapes=[pltpu.SemaphoreType.DMA((count, cuts))],
        compiler_params=pltpu.CompilerParams(vmem_limit_bytes=2 * MIB),
        cost_estimate=pl.CostEstimate(flops=1024, bytes_accessed=1024, transcendentals=0),
    )(target, pltpu.with_memory_space_constraint(weights, pltpu.HBM))


def encode_kernel(count, *refs):
    pieces, (w_ref, b_ref, out_ref) = refs[:count], refs[count:]
    rows = jnp.concatenate([piece[...] for piece in pieces], 0)
    pre = jnp.dot(rows, w_ref[...], preferred_element_type=F32) + b_ref[...]
    out_ref[...] = jnp.maximum(pre, 0.0).astype(BF16)


def encode(pieces, w, b):
    count = len(pieces)
    rows = sum(piece.shape[0] for piece in pieces)
    depth, wide = w.shape
    return pl.pallas_call(
        functools.partial(encode_kernel, count),
        in_specs=[WHOLE] * (count + 2),
        out_specs=WHOLE,
        out_shape=pltpu.VMEM((rows, wide), BF16),
        compiler_params=pltpu.CompilerParams(vmem_limit_bytes=16 * MIB),
        cost_estimate=pl.CostEstimate(flops=1024, bytes_accessed=1024, transcendentals=0),
    )(*pieces, w, b)


def decode_kernel(count, tile, summed, halved, *refs):
    lats, ws, rest = refs[:count], refs[count : 2 * count], refs[2 * count :]
    wide = ws[0].shape[1]

    @pl.loop(0, wide // tile)
    def _(n):
        columns = pl.ds(pl.multiple_of(n * tile, tile), tile)
        total = jnp.dot(lats[0][...], ws[0][:, columns], preferred_element_type=F32)
        for lat, w in zip(lats[1:], ws[1:]):
            total += jnp.dot(lat[...], w[:, columns], preferred_element_type=F32)
        if summed:
            total += rest[0][:, columns]
        if halved:
            top_ref, low_ref = rest[-2:]
            half = top_ref.shape[0]
            top_ref[:, columns] = total[:half]
            low_ref[:, columns] = total[half:].astype(BF16)
        else:
            rest[-1][:, columns] = total


def decode(lats, weights, acc=None, halved=False):
    count = len(lats)
    rows, depth = lats[0].shape
    wide = weights[0].shape[1]
    summed = acc is not None
    halves = [pltpu.VMEM((rows // 2, wide), F32), pltpu.VMEM((rows // 2, wide), BF16)]
    return pl.pallas_call(
        functools.partial(decode_kernel, count, tile_of(wide, 4096), summed, halved),
        in_specs=[WHOLE] * (2 * count + summed),
        out_specs=[WHOLE, WHOLE] if halved else WHOLE,
        out_shape=halves if halved else pltpu.VMEM((rows, wide), F32),
        compiler_params=pltpu.CompilerParams(vmem_limit_bytes=8 * MIB),
        cost_estimate=pl.CostEstimate(flops=1024, bytes_accessed=1024, transcendentals=0),
    )(*lats, *weights, *([acc] if summed else []))


def body(resid, mlp_out, enc_w, enc_b, dec_w):
    target = lax.axis_index("layer").reshape(1)
    layers = lax.axis_size("layer")
    peers = lax.axis_size("latent")
    bits = [1 << bit for bit in range(1, peers.bit_length() - 1)]
    steps = list(zip(bits, bits[::-1]))

    encoder, bias, mine = load([enc_w[0], enc_b, resid[0]], [4, 1, 1])
    pieces = [resid[0]]
    for step, masks in enumerate(steps):
        pieces += [swap(piece, masks) for piece in ([mine] + pieces[1:] if step else pieces)]
    pieces[0] = mine
    half = len(pieces) // 2

    mates = [swap(piece, (1, 1)) for piece in pieces[:half]]
    near = [encode(pieces[:half] + mates, encoder, bias)]
    mates = [swap(piece, (1, 1)) for piece in pieces[half:]]
    far = [encode(pieces[half:] + [after(mates[0], near[0])] + mates[1:], encoder, bias)]
    weights = pick(after(dec_w[0], far[0]), target)
    for held in (near, far):
        for j in range(1, layers):
            if j % 2:
                held.append(up(held[-1] if j == 1 else after(held[-1], weights[0]), 1, j))
            else:
                held.append(up(held[j - 2], 2, j))

    near_sum = decode(near[:-1], weights[:-1])
    far_sum = decode([after(lat, far[-2]) for lat in far[:-1]], weights[:-1])
    top, low = decode(near[-1:], weights[-1:], near_sum, True)
    ends = [top + swap(low, (1, 1)).astype(F32)]
    top, low = decode([after(far[-1], low)], weights[-1:], far_sum, True)
    ends.append(top + swap(low, (1, 1)).astype(F32))
    each = resid.shape[1]
    totals = [end[i * each : (i + 1) * each] for end in ends for i in range(half)]
    for masks in steps[::-1]:
        half = len(totals) // 2
        for i in reversed(range(half)):
            totals[i] = totals[i] + swap(totals[half + i].astype(BF16), masks).astype(F32)
        totals = totals[:half]
    return (mlp_out[0].astype(F32) - totals[0]).astype(BF16)[None]


def solution(mesh):
    return jax.shard_map(
        body,
        mesh=mesh,
        in_specs=(
            P("layer", "latent", None),
            P("layer", "latent", None),
            P("layer", None, "latent"),
            P("layer", "latent"),
            P("layer", None, "latent", None),
        ),
        out_specs=P("layer", "latent", None),
        check_vma=False,
    )
```
